256 devices in a mesh: row: 32 (over z, x), col: 8 (over y, core).
Axes of the slice: x: 4, y: 4, z: 8, core: 2. Of those that a mesh axis runs over, the one named last changes fastest.
Arguments:
- modes: float32 [131072, 2048], P('row', 'col'), may hold values from -6 to 6
- panel_one: float32 [131072, 256], P('row', 'col'), may hold values from -0.015625 to 0.015625
- panel_two: float32 [131072, 256], P('row', 'col'), may hold values from -0.015625 to 0.015625
- factor_one: float32 [256, 256], replicated, may hold values from -1 to 2, as said below
- factor_two: float32 [256, 256], replicated, may hold values from -1 to 2, as said below
Outputs:
- updated: float32 [131072, 2048], P('row', 'col')
- coordinates: float32 [512, 2048], P(None, 'col')
The draws below stay inside these ranges and needn't reach their ends.
Inputs may be any that keep to these rules, and one draw needn't show every extreme that they name: factor_one is upper triangular with diagonal entries between 1 and 2. factor_two is upper triangular with diagonal entries between 1 and 2.
All inputs are finite; a program needn't handle non-finite values.
Results may differ from the reference program's by a relative error of at most 0.000086.
Values sent between devices are 32-bit elements; how exact they have to be, the bound alone decides.
A program may use at most 64 MiB of HBM per device.

```python
import jax
import jax.numpy as jnp
from jax import lax

M = 2048
NB = 256
N = 131072


def make_factor(key):
    key_diag, key_off = jax.random.split(key)
    diagonal = jax.random.uniform(key_diag, (NB,), jnp.float32, 1.0, 2.0)
    spread = 0.5 / jnp.sqrt(jnp.float32(NB))
    offdiag = jnp.clip(jax.random.normal(key_off, (NB, NB), jnp.float32) * spread, -0.9, 0.9)
    rows = index_rows(NB)
    upper = rows[None, :] > rows[:, None]
    return jnp.where(upper, offdiag, 0.0) + jnp.diag(diagonal)


def index_rows(count):
    return jnp.arange(count, dtype=jnp.int32)


def draw_factor_one(key, part):
    key = jax.random.fold_in(key, 11)
    return make_factor(key)


def draw_factor_two(key, part):
    key = jax.random.fold_in(key, 23)
    return make_factor(key)


def shard_levels(stream_key, dims, cuts, least, largest):
    def one(dim, shards_of):
        draws = jax.random.uniform(jax.random.fold_in(jax.random.fold_in(stream_key, 6), dim), (shards_of,), jnp.float32, least / len(cuts), largest / len(cuts))
        return jnp.repeat(jnp.exp(draws), dims[dim] // shards_of).reshape((-1,) + (1,) * (len(dims) - dim - 1))

    level = one(*cuts[0])
    for cut in cuts[1:]:
        level = level * one(*cut)
    return level


def bell_draw(key, extent, width, bound, shards=(), kind=jnp.bfloat16):
    array = jax.random.normal(key, extent, jnp.float32) * width
    if len(shards) > 0:
        array = shard_levels(key, extent, shards, -0.22, 0.18) * array
    return jnp.clip(array, min=-bound, max=bound).astype(kind)


def setup_inputs(seed: int = 0) -> dict:
    seeds = jax.random.split(jax.random.key(seed), 6)
    modes = bell_draw(seeds[0], (N, M), 1.0, 6.0, ((0, 32), (1, 8)), jnp.float32)
    panel_one = bell_draw(seeds[1], (N, NB), N ** -0.5, 0.015625, ((0, 32), (1, 8)), jnp.float32)
    panel_two = bell_draw(seeds[2], (N, NB), N ** -0.5, 0.015625, ((0, 32), (1, 8)), jnp.float32)
    factor_one = draw_factor_one(jax.random.fold_in(seeds[5], 71), 0)
    factor_two = draw_factor_two(jax.random.fold_in(seeds[5], 71), 0)
    return {"modes": modes, "panel_one": panel_one, "panel_two": panel_two, "factor_one": factor_one, "factor_two": factor_two}


precise = lax.Precision.HIGHEST


def contract(left, right):
    return lax.dot_general(left, right, (((0,), (0,)), ((), ())), precision=precise, preferred_element_type=jnp.float32)


def product(left, right):
    return jnp.dot(left, right, precision=precise, preferred_element_type=jnp.float32)


def reference(modes, panel_one, panel_two, factor_one, factor_two):
    coord_two = product(factor_two, contract(panel_two, modes))
    middle = modes - product(panel_two, coord_two)
    coord_one = product(factor_one, contract(panel_one, middle))
    updated = middle - product(panel_one, coord_one)
    return updated, jnp.concatenate([coord_one, coord_two], axis=0)
```

```python
import functools

import jax
import jax.numpy as jnp
from jax import lax
from jax.experimental import pallas as pl
from jax.experimental.pallas import tpu as pltpu
from jax.sharding import PartitionSpec as P

MESH = pl.DeviceIdType.MESH
F32, BF16 = jnp.float32, jnp.bfloat16
ROWS, COLS, NB = 4096, 256, 256
SHARE = 32
UNITS, UNIT = 4, 8
HALF = ROWS // 2
NX, NY, NZ = 4, 4, 8
GRAM = 8
STEP = 1024
PLACE = {0: 0, 1: 1, 3: 2, 2: 3}
AWAY = [0, 1, 3, 2]


def split(value):
    high = value.astype(BF16)
    return high, (value - high.astype(F32)).astype(BF16)


def dot(a, b):
    return jnp.dot(a, b, preferred_element_type=F32)


def exact(a, b):
    return jnp.dot(a, b, precision=lax.Precision.HIGHEST, preferred_element_type=F32)


def kernel(
    modes, panel_one, panel_two, factor_one, factor_two, updated, coords,
    work, gathered, mode_high, mode_low, high, low, factors, part, from_x, from_z, sums, gram, right_side,
    load_sem, own_send, own_recv, fwd_send, fwd_recv, sib_send, sib_recv,
    x_send, x_recv, z_send, z_recv, back_send, back_recv, gram_send, gram_recv, gsib_send, gsib_recv, out_sem,
):
    row, col = lax.axis_index("row"), lax.axis_index("col")
    z, x, y, k = row // NX, row % NX, col // 2, col % 2
    up, down = (row, lax.rem(y + 1, NY) * 2 + k), (row, lax.rem(y + NY - 1, NY) * 2 + k)
    sibling = (row, y * 2 + 1 - k)
    across = (row, lax.rem(y + 2, NY) * 2 + k)
    x_peer = [None] + [(z * NX + lax.rem(x + d, NX), col) for d in range(1, NX)]
    z_peer = [None] + [(lax.rem(z + d, NZ) * NX + x, col) for d in range(1, NZ)]
    panels = (panel_two, panel_one)
    mine = pl.ds(pl.multiple_of(k * SHARE, SHARE), SHARE)
    sends = []

    def remote(src, dst, send, recv, device):
        copy = pltpu.make_async_remote_copy(
            src_ref=src, dst_ref=dst, send_sem=send, recv_sem=recv, device_id=device, device_id_type=MESH
        )
        copy.start()
        sends.append(copy)
        return copy

    loads = []
    for p in range(2):
        loads.append(pltpu.make_async_copy(panels[p], gathered.at[p, mine], load_sem.at[p]))
    for i in range(8):
        rows = pl.ds(i * 512, 512)
        loads.append(pltpu.make_async_copy(modes.at[rows], work.at[rows], load_sem.at[4 + i]))
    loads.append(pltpu.make_async_copy(factor_two, factors.at[0], load_sem.at[2]))
    loads.append(pltpu.make_async_copy(factor_one, factors.at[1], load_sem.at[3]))
    for copy in loads:
        copy.start()

    barrier = pltpu.get_barrier_semaphore()
    friends = [up, down, across, sibling] + x_peer[1:] + z_peer[1:]
    for device in friends:
        pl.semaphore_signal(barrier, inc=1, device_id=device, device_id_type=MESH)
    pl.semaphore_wait(barrier, len(friends))

    def unit_rows(place, u):
        return pl.ds(pl.multiple_of(place * 64 + k * SHARE + u * UNIT, UNIT), UNIT)

    def send_own(p):
        got = {}
        for u in range(UNITS):
            src = panels[p].at[pl.ds(u * UNIT, UNIT)]
            for way, (device, away) in enumerate(((up, 3), (down, 1))):
                got[way, u] = remote(
                    src, gathered.at[p, unit_rows(PLACE[away], u)], own_send.at[p, way, u], own_recv.at[p, way, u], device
                )
        return got

    def to_sibling(p, place, u):
        rows = unit_rows(place, u)
        return remote(
            gathered.at[p, rows], gathered.at[p, rows], sib_send.at[p, place, u], sib_recv.at[p, place, u], sibling
        )

    def pass_on(p, own, u):
        copies = []
        for way, (device, away) in enumerate(((up, 3), (down, 1))):
            own[way, u].wait_recv()
            lanes = pl.ds(way * HALF, HALF)
            copies.append(remote(
                gathered.at[p, unit_rows(PLACE[away], u), lanes], gathered.at[p, unit_rows(3, u), lanes],
                fwd_send.at[p, way, u], fwd_recv.at[p, way, u], device,
            ))
        return copies, [to_sibling(p, PLACE[away], u) for away in (3, 1)]

    def multiply(p, place, group):
        total = jnp.zeros((64, COLS), F32)
        for i in range(ROWS // STEP):
            lanes = slice(i * STEP, (i + 1) * STEP)
            h, l = split(gathered[p, place * 64:(place + 1) * 64, lanes])
            two = dot(jnp.concatenate([h, l], axis=0), mode_high[lanes])
            total += two[:64] + two[64:] + dot(h, mode_low[lanes])
        part[group] = total

    def turn(p, pair):
        for i in range(ROWS // STEP):
            lanes = slice(i * STEP, (i + 1) * STEP)
            h, l = split(gathered[p, pair * 128:(pair + 1) * 128, lanes].T)
            high[p, lanes, pair * 128:(pair + 1) * 128] = h
            low[p, lanes, pair * 128:(pair + 1) * 128] = l

    class Group:
        def __init__(self, group, count, target, base):
            self.group, self.m, self.target, self.base = group, count // NX, target, base

        def piece(self, at):
            return pl.ds(pl.multiple_of(at * self.m, self.m), self.m)

        def share_out(self):
            g, m = self.group, self.m
            self.copies = [
                remote(part.at[g, self.piece(lax.rem(x + d, NX))], from_x.at[g, d - 1, pl.ds(0, m)],
                       x_send.at[g, d - 1], x_recv.at[g, d - 1], x_peer[d])
                for d in range(1, NX)
            ]

        def exchange(self):
            g, m = self.group, self.m
            for copy in self.copies:
                copy.wait_recv()
            from_z[g, z, 0:m] = part[g, self.piece(x)] + from_x[g, 0, 0:m] + from_x[g, 1, 0:m] + from_x[g, 2, 0:m]
            self.copies = [
                remote(from_z.at[g, z, pl.ds(0, m)], from_z.at[g, z, pl.ds(0, m)],
                       z_send.at[g, d - 1], z_recv.at[g, d - 1], z_peer[d])
                for d in range(1, NZ)
            ]

        def collect(self):
            g, m = self.group, self.m
            for copy in self.copies:
                copy.wait_recv()
            total = from_z[g, 0, 0:m]
            for i in range(1, NZ):
                total += from_z[g, i, 0:m]
            rows = pl.ds(pl.multiple_of(self.base + x * m, m), m)
            self.target[rows] = total
            self.copies = [
                remote(self.target.at[rows], self.target.at[rows], back_send.at[g, d - 1], back_recv.at[g, d - 1], x_peer[d])
                for d in range(1, NX)
            ]

        def finish(self):
            for copy in self.copies:
                copy.wait_recv()

    def y_of(place):
        return lax.rem(y + AWAY[place], NY)

    groups = {
        (p, s): Group(p * 4 + s, 64, sums.at[p], pl.multiple_of(y_of(s) * 64, 64)) for p in range(2) for s in range(4)
    }
    gram_group = Group(GRAM, SHARE, gram, pl.multiple_of(k * SHARE, SHARE))

    def local(value, home):
        return jnp.concatenate(
            [value[pl.ds(pl.multiple_of(lax.rem(home + AWAY[s], NY) * 64, 64), 64)] for s in range(4)], axis=0
        )

    own_two = send_own(0)
    sib_own = []
    for p in range(2):
        for u in range(UNITS):
            rows = unit_rows(0, u)
            sib_own.append(remote(
                panels[p].at[pl.ds(u * UNIT, UNIT)], gathered.at[p, rows], sib_send.at[p, 0, u], sib_recv.at[p, 0, u], sibling
            ))
    for copy in loads:
        copy.wait()
    for i in range(8):
        rows = slice(i * 512, (i + 1) * 512)
        mode_high[rows], mode_low[rows] = split(work[rows])
    for copy in sib_own:
        copy.wait_recv()
    for p in range(2):
        multiply(p, 0, p * 4)
        groups[p, 0].share_out()

    passed, siblings = [], []

    def relay(p, own, u):
        a, b = pass_on(p, own, u)
        passed.append(a)
        siblings.extend(b)

    relay(0, own_two, 0)
    for p in range(2):
        groups[p, 0].exchange()
    relay(0, own_two, 1)
    relay(0, own_two, 2)
    for p in range(2):
        groups[p, 0].collect()
    relay(0, own_two, 3)
    own_one = send_own(1)
    for copy in siblings:
        copy.wait_recv()
    passed_two, passed, siblings = passed, [], []
    for s in (1, 2):
        multiply(0, s, s)
        groups[0, s].share_out()
    turn(0, 0)
    last = []
    for u in range(UNITS):
        for copy in passed_two[u]:
            copy.wait_recv()
        last.append(to_sibling(0, 3, u))
    for s in (1, 2):
        groups[0, s].exchange()
    for copy in last:
        copy.wait_recv()
    multiply(0, 3, 3)
    groups[0, 3].share_out()
    turn(0, 1)
    relay(1, own_one, 0)

    total = jnp.zeros((SHARE, NB), F32)
    for i in range(ROWS // STEP):
        lanes = slice(i * STEP, (i + 1) * STEP)
        h, l = split(gathered[1, mine, lanes])
        two = dot(jnp.concatenate([h, l], axis=0), high[0, lanes])
        total += two[:SHARE] + two[SHARE:] + dot(h, low[0, lanes])
    part[GRAM, 0:SHARE] = total
    gram_group.share_out()
    groups[0, 3].exchange()
    for s in (1, 2):
        groups[0, s].collect()
    relay(1, own_one, 1)
    gram_group.exchange()
    groups[0, 3].collect()
    relay(1, own_one, 2)
    gram_group.collect()
    relay(1, own_one, 3)
    for copy in siblings:
        copy.wait_recv()
    for s in (1, 2):
        multiply(1, s, 4 + s)
        groups[1, s].share_out()
    turn(1, 0)
    last = []
    for u in range(UNITS):
        for copy in passed[u]:
            copy.wait_recv()
        last.append(to_sibling(1, 3, u))
    for s in (1, 2):
        groups[1, s].exchange()
    for copy in last:
        copy.wait_recv()
    multiply(1, 3, 7)
    groups[1, 3].share_out()
    turn(1, 1)
    gram_group.finish()
    around = [
        remote(gram.at[mine], gram.at[pl.ds(pl.multiple_of(away * 64 + k * SHARE, SHARE), SHARE)],
               gram_send.at[away], gram_recv.at[away], device)
        for away, device in ((3, up), (1, down), (2, across))
    ]
    for s in range(4):
        groups[0, s].finish()
    coord_two = exact(factors[0], sums[0])
    coords[NB:2 * NB] = coord_two
    groups[1, 3].exchange()
    for s in (1, 2):
        groups[1, s].collect()
    for copy in around:
        copy.wait_recv()
    swap = []
    for away in range(4):
        rows = pl.ds(pl.multiple_of(away * 64 + k * SHARE, SHARE), SHARE)
        swap.append(remote(gram.at[rows], gram.at[rows], gsib_send.at[away], gsib_recv.at[away], sibling))

    def update(p, c, emit):
        ch, cl = split(c)
        for i in range(8):
            rows = slice(i * 512, (i + 1) * 512)
            h = high[p, rows]
            emit(rows, work[rows] - (dot(h, ch) + dot(low[p, rows], ch) + dot(h, cl)))

    def keep(rows, value):
        work[rows] = value

    two_at = coords.at[NB:2 * NB]
    update(0, local(two_at, y), keep)
    for copy in swap:
        copy.wait_recv()
    for away in range(4):
        home = lax.rem(y + away, NY)
        right_side[pl.ds(pl.multiple_of(home * 64, 64), 64)] = exact(gram[away * 64:(away + 1) * 64], local(two_at, home))
    groups[1, 3].collect()
    for s in range(4):
        groups[1, s].finish()
    coords[0:NB] = exact(factors[1], sums[1] - right_side[...])
    outs = []

    def emit(rows, value):
        work[rows] = value
        copy = pltpu.make_async_copy(work.at[rows], updated.at[rows], out_sem.at[rows.start // 512])
        copy.start()
        outs.append(copy)

    update(1, local(coords.at[0:NB], y), emit)
    for copy in sends:
        copy.wait_send()
    for copy in outs:
        copy.wait()


def shards(modes, panel_one, panel_two, factor_one, factor_two):
    hbm = pl.BlockSpec(memory_space=pltpu.HBM)
    dma = pltpu.SemaphoreType.DMA
    return pl.pallas_call(
        kernel,
        out_shape=(jax.ShapeDtypeStruct((ROWS, COLS), F32), jax.ShapeDtypeStruct((2 * NB, COLS), F32)),
        in_specs=[hbm] * 5,
        out_specs=(hbm, pl.BlockSpec(memory_space=pltpu.VMEM)),
        scratch_shapes=[
            pltpu.VMEM((ROWS, COLS), F32),
            pltpu.VMEM((2, NB, ROWS), F32),
            pltpu.VMEM((ROWS, COLS), BF16),
            pltpu.VMEM((ROWS, COLS), BF16),
            pltpu.VMEM((2, ROWS, NB), BF16),
            pltpu.VMEM((2, ROWS, NB), BF16),
            pltpu.VMEM((2, NB, NB), F32),
            pltpu.VMEM((9, 64, COLS), F32),
            pltpu.VMEM((9, NX - 1, 16, COLS), F32),
            pltpu.VMEM((9, NZ, 16, COLS), F32),
            pltpu.VMEM((2, NB, COLS), F32),
            pltpu.VMEM((NB, NB), F32),
            pltpu.VMEM((NB, COLS), F32),
            dma((12,)),
            dma((2, 2, UNITS)), dma((2, 2, UNITS)),
            dma((2, 2, UNITS)), dma((2, 2, UNITS)),
            dma((2, 4, UNITS)), dma((2, 4, UNITS)),
            dma((9, NX - 1)), dma((9, NX - 1)),
            dma((9, NZ - 1)), dma((9, NZ - 1)),
            dma((9, NX - 1)), dma((9, NX - 1)),
            dma((4,)), dma((4,)),
            dma((4,)), dma((4,)),
            dma((8,)),
        ],
        compiler_params=pltpu.CompilerParams(collective_id=0, has_side_effects=True, vmem_limit_bytes=56 << 20),
    )(modes, panel_one.T, panel_two.T, factor_one, factor_two)


def solution(mesh):
    return jax.shard_map(
        shards,
        mesh=mesh,
        in_specs=(P("row", "col"), P("row", "col"), P("row", "col"), P(), P()),
        out_specs=(P("row", "col"), P(None, "col")),
        check_vma=False,
    )
```

```python
import functools

import jax
import jax.numpy as jnp
from jax import lax
from jax.experimental import pallas as pl
from jax.experimental.pallas import tpu as pltpu
from jax.sharding import PartitionSpec as P

MESH = pl.DeviceIdType.MESH
F32, BF16 = jnp.float32, jnp.bfloat16
ROWS, COLS, NB = 4096, 256, 256
SHARE = 32
UNITS, UNIT = 4, 8
HALF = ROWS // 2
NX, NY, NZ = 4, 4, 8
GRAM = 10
STEP = 1024
PLACE = {0: 0, 1: 1, 3: 2, 2: 3}
AWAY = [0, 1, 3, 2]


def split(value):
    high = value.astype(BF16)
    return high, (value - high.astype(F32)).astype(BF16)


def dot(a, b):
    return jnp.dot(a, b, preferred_element_type=F32)


def exact(a, b):
    return jnp.dot(a, b, precision=lax.Precision.HIGHEST, preferred_element_type=F32)


def kernel(
    modes, panel_one, panel_two, factor_one, factor_two, work, coords,
    gathered, mode_high, mode_low, high, low, factors, part, from_x, from_z, sums, gram, right_side,
    load_sem, own_send, own_recv, fwd_send, fwd_recv, sib_send, sib_recv,
    x_send, x_recv, z_send, z_recv, back_send, back_recv, gram_send, gram_recv, gsib_send, gsib_recv,
):
    row, col = lax.axis_index("row"), lax.axis_index("col")
    z, x, y, k = row // NX, row % NX, col // 2, col % 2
    up, down = (row, lax.rem(y + 1, NY) * 2 + k), (row, lax.rem(y + NY - 1, NY) * 2 + k)
    sibling = (row, y * 2 + 1 - k)
    across = (row, lax.rem(y + 2, NY) * 2 + k)
    x_peer = [None] + [(z * NX + lax.rem(x + d, NX), col) for d in range(1, NX)]
    z_peer = [None] + [(lax.rem(z + d, NZ) * NX + x, col) for d in range(1, NZ)]
    panels = (panel_two, panel_one)
    mine = pl.ds(pl.multiple_of(k * SHARE, SHARE), SHARE)
    sends = []

    def remote(src, dst, send, recv, device):
        copy = pltpu.make_async_remote_copy(
            src_ref=src, dst_ref=dst, send_sem=send, recv_sem=recv, device_id=device, device_id_type=MESH
        )
        copy.start()
        sends.append(copy)
        return copy

    loads = []
    for p in range(2):
        loads.append(pltpu.make_async_copy(panels[p], gathered.at[p, mine], load_sem.at[p]))
    for i in range(8):
        rows = pl.ds(i * 512, 512)
        loads.append(pltpu.make_async_copy(modes.at[rows], work.at[rows], load_sem.at[4 + i]))
    loads.append(pltpu.make_async_copy(factor_two, factors.at[0], load_sem.at[2]))
    loads.append(pltpu.make_async_copy(factor_one, factors.at[1], load_sem.at[3]))
    for copy in loads:
        copy.start()

    barrier = pltpu.get_barrier_semaphore()
    friends = [up, down, across, sibling] + x_peer[1:] + z_peer[1:]
    for device in friends:
        pl.semaphore_signal(barrier, inc=1, device_id=device, device_id_type=MESH)
    pl.semaphore_wait(barrier, len(friends))

    def unit_rows(place, u):
        return pl.ds(pl.multiple_of(place * 64 + k * SHARE + u * UNIT, UNIT), UNIT)

    def send_own(p):
        got = {}
        for u in range(UNITS):
            src = panels[p].at[pl.ds(u * UNIT, UNIT)]
            for way, (device, away) in enumerate(((up, 3), (down, 1))):
                got[way, u] = remote(
                    src, gathered.at[p, unit_rows(PLACE[away], u)], own_send.at[p, way, u], own_recv.at[p, way, u], device
                )
        return got

    def to_sibling(p, place, u):
        rows = unit_rows(place, u)
        return remote(
            gathered.at[p, rows], gathered.at[p, rows], sib_send.at[p, place, u], sib_recv.at[p, place, u], sibling
        )

    def pass_on(p, own, u):
        copies = []
        for way, (device, away) in enumerate(((up, 3), (down, 1))):
            own[way, u].wait_recv()
            lanes = pl.ds(way * HALF, HALF)
            copies.append(remote(
                gathered.at[p, unit_rows(PLACE[away], u), lanes], gathered.at[p, unit_rows(3, u), lanes],
                fwd_send.at[p, way, u], fwd_recv.at[p, way, u], device,
            ))
        return copies, [to_sibling(p, PLACE[away], u) for away in (3, 1)]

    def multiply(p, slices, group):
        count = sum(n for _, n in slices)
        total = jnp.zeros((count, COLS), F32)
        for i in range(ROWS // STEP):
            lanes = slice(i * STEP, (i + 1) * STEP)
            rows = [gathered[p, at:at + n, lanes] for at, n in slices]
            h, l = split(rows[0] if len(rows) == 1 else jnp.concatenate(rows, axis=0))
            two = dot(jnp.concatenate([h, l], axis=0), mode_high[lanes])
            total += two[:count] + two[count:] + dot(h, mode_low[lanes])
        part[group, 0:count] = total

    def turn(p, pair):
        for i in range(ROWS // STEP):
            lanes = slice(i * STEP, (i + 1) * STEP)
            h, l = split(gathered[p, pair * 128:(pair + 1) * 128, lanes].T)
            high[p, lanes, pair * 128:(pair + 1) * 128] = h
            low[p, lanes, pair * 128:(pair + 1) * 128] = l

    class Group:
        def __init__(self, group, m, target, base):
            self.group, self.m, self.target, self.base = group, m, target, base

        def piece(self, at):
            return pl.ds(pl.multiple_of(at * self.m, self.m), self.m)

        def share_out(self):
            g, m = self.group, self.m
            self.copies = [
                remote(part.at[g, self.piece(lax.rem(x + d, NX))], from_x.at[g, d - 1, pl.ds(0, m)],
                       x_send.at[g, d - 1], x_recv.at[g, d - 1], x_peer[d])
                for d in range(1, NX)
            ]

        def to_z(self, value):
            g, m = self.group, self.m
            from_z[g, z, 0:m] = value
            self.copies = [
                remote(from_z.at[g, z, pl.ds(0, m)], from_z.at[g, z, pl.ds(0, m)],
                       z_send.at[g, d - 1], z_recv.at[g, d - 1], z_peer[d])
                for d in range(1, NZ)
            ]

        def exchange(self):
            g, m = self.group, self.m
            self.finish()
            self.to_z(part[g, self.piece(x)] + from_x[g, 0, 0:m] + from_x[g, 1, 0:m] + from_x[g, 2, 0:m])

        def z_sum(self):
            self.finish()
            total = from_z[self.group, 0, 0:self.m]
            for i in range(1, NZ):
                total += from_z[self.group, i, 0:self.m]
            return total

        def collect(self):
            g = self.group
            rows = pl.ds(pl.multiple_of(self.base, self.m), self.m)
            self.target[rows] = self.z_sum()
            self.copies = [
                remote(self.target.at[rows], self.target.at[rows], back_send.at[g, d - 1], back_recv.at[g, d - 1], x_peer[d])
                for d in range(1, NX)
            ]

        def finish(self):
            for copy in self.copies:
                copy.wait_recv()

    class Short(Group):
        def share_out(self):
            g = self.group
            from_x[g, x] = part[g, 0:16]
            self.copies = [
                remote(from_x.at[g, x], from_x.at[g, x], x_send.at[g, d - 1], x_recv.at[g, d - 1], x_peer[d])
                for d in range(1, NX)
            ]

        def exchange(self):
            g = self.group
            self.finish()
            self.to_z(((from_x[g, 0] + from_x[g, 1]) + from_x[g, 2]) + from_x[g, 3])

        def collect(self):
            total = self.z_sum()
            for core in range(2):
                self.target[pl.ds(pl.multiple_of(self.base + core * SHARE, UNIT), UNIT)] = total[core * UNIT:(core + 1) * UNIT]

    def block(away):
        return lax.rem(y + away, NY) * 64

    own = [Group(p, 16, sums.at[p], block(0) + x * 16) for p in range(2)]
    near = [
        [Group(2 + 2 * p + h, 16, sums.at[p], block(1 + 2 * (x // 2)) + (x % 2) * SHARE + h * 16) for h in range(2)]
        for p in range(2)
    ]
    far_two = Group(6, 16, sums.at[0], block(2) + x * 16)
    far_one = Group(7, 8, sums.at[1], block(2) + (x // 2) * SHARE + (x % 2) * UNIT)
    tail = [Short(8 + i, 16, sums.at[1], block(2) + (2 + i) * UNIT) for i in range(2)]
    gram_group = Group(GRAM, 8, gram, k * SHARE + x * 8)

    def near_rows(h):
        return [(place * 64 + core * SHARE + h * 16, 16) for place in (1, 2) for core in range(2)]

    def local(value, home):
        return jnp.concatenate(
            [value[pl.ds(pl.multiple_of(lax.rem(home + AWAY[s], NY) * 64, 64), 64)] for s in range(4)], axis=0
        )

    own_two = send_own(0)
    sib_own = []
    for p in range(2):
        for u in range(UNITS):
            rows = unit_rows(0, u)
            sib_own.append(remote(
                panels[p].at[pl.ds(u * UNIT, UNIT)], gathered.at[p, rows], sib_send.at[p, 0, u], sib_recv.at[p, 0, u], sibling
            ))
    for copy in loads:
        copy.wait()
    for i in range(8):
        rows = slice(i * 512, (i + 1) * 512)
        mode_high[rows], mode_low[rows] = split(work[rows])
    for copy in sib_own:
        copy.wait_recv()
    for p in range(2):
        multiply(p, [(0, 64)], p)
        own[p].share_out()

    def relay(p, sent, u):
        copies, swaps = pass_on(p, sent, u)
        return copies, swaps

    def wait(copies):
        for copy in copies:
            copy.wait_recv()

    def far_unit(p, copies, u):
        wait(copies)
        return to_sibling(p, 3, u)

    def gram_part():
        total = jnp.zeros((SHARE, NB), F32)
        for i in range(ROWS // STEP):
            lanes = slice(i * STEP, (i + 1) * STEP)
            h, l = split(gathered[1, mine, lanes])
            two = dot(jnp.concatenate([h, l], axis=0), high[0, lanes])
            total += two[:SHARE] + two[SHARE:] + dot(h, low[0, lanes])
        part[GRAM, 0:SHARE] = total

    def update(p, c, chunks):
        ch, cl = split(c)
        for i in chunks:
            rows = slice(i * 512, (i + 1) * 512)
            h = high[p, rows]
            work[rows] = work[rows] - (dot(h, ch) + dot(low[p, rows], ch) + dot(h, cl))

    on, swaps = [None] * UNITS, [None] * UNITS
    on[0], swaps[0] = relay(0, own_two, 0)
    own[0].exchange()
    own[1].exchange()
    on[1], swaps[1] = relay(0, own_two, 1)
    wait(swaps[0] + swaps[1])
    multiply(0, near_rows(0), near[0][0].group)
    near[0][0].share_out()
    on[2], swaps[2] = relay(0, own_two, 2)
    on[3], swaps[3] = relay(0, own_two, 3)
    own_one = send_own(1)
    near[0][0].exchange()
    wait(swaps[2] + swaps[3])
    multiply(0, near_rows(1), near[0][1].group)
    near[0][1].share_out()
    own[0].collect()
    own[1].collect()
    turn(0, 0)
    far = [far_unit(0, on[u], u) for u in range(UNITS)]
    near[0][1].exchange()
    wait(far)
    multiply(0, [(192, 64)], far_two.group)
    far_two.share_out()
    turn(0, 1)
    on[0], swaps[0] = relay(1, own_one, 0)
    gram_part()
    gram_group.share_out()
    near[0][0].collect()
    on[1], swaps[1] = relay(1, own_one, 1)
    far_two.exchange()
    wait(swaps[0] + swaps[1])
    multiply(1, near_rows(0), near[1][0].group)
    near[1][0].share_out()
    near[0][1].collect()
    on[2], swaps[2] = relay(1, own_one, 2)
    gram_group.exchange()
    on[3], swaps[3] = relay(1, own_one, 3)
    near[1][0].exchange()
    wait(swaps[2] + swaps[3])
    multiply(1, near_rows(1), near[1][1].group)
    near[1][1].share_out()
    far_two.collect()
    turn(1, 0)
    far = [far_unit(1, on[u], u) for u in range(2)]
    gram_group.collect()
    wait(far)
    multiply(1, [(192, 16), (224, 16)], far_one.group)
    far_one.share_out()
    far = [far_unit(1, on[2], 2)]
    for group in (own[0], near[0][0], near[0][1], far_two):
        group.finish()
    coords[NB:2 * NB] = exact(factors[0], sums[0])
    wait(far)
    multiply(1, [(208, 8), (240, 8)], tail[0].group)
    tail[0].share_out()
    near[1][1].exchange()
    far = [far_unit(1, on[3], 3)]
    wait(far)
    multiply(1, [(216, 8), (248, 8)], tail[1].group)
    tail[1].share_out()
    near[1][0].collect()
    far_one.exchange()
    gram_group.finish()
    around = [
        remote(gram.at[mine], gram.at[pl.ds(pl.multiple_of(away * 64 + k * SHARE, SHARE), SHARE)],
               gram_send.at[away], gram_recv.at[away], device)
        for away, device in ((3, up), (1, down), (2, across))
    ]
    two_at = coords.at[NB:2 * NB]
    near_two = local(two_at, y)
    tail[0].exchange()
    update(0, near_two, range(0, 3))
    tail[1].exchange()
    update(0, near_two, range(3, 8))
    near[1][1].collect()
    wait(around)
    swap = []
    for away in range(4):
        rows = pl.ds(pl.multiple_of(away * 64 + k * SHARE, SHARE), SHARE)
        swap.append(remote(gram.at[rows], gram.at[rows], gsib_send.at[away], gsib_recv.at[away], sibling))
    turn(1, 1)
    far_one.collect()
    wait(swap)
    for away in range(4):
        home = lax.rem(y + away, NY)
        right_side[pl.ds(pl.multiple_of(home * 64, 64), 64)] = exact(gram[away * 64:(away + 1) * 64], local(two_at, home))
    for group in (own[1], near[1][0], near[1][1], far_one):
        group.finish()
    tail[0].collect()
    tail[1].collect()
    coords[0:NB] = exact(factors[1], sums[1] - right_side[...])
    update(1, local(coords.at[0:NB], y), range(8))
    for copy in sends:
        copy.wait_send()


def shards(modes, panel_one, panel_two, factor_one, factor_two):
    hbm = pl.BlockSpec(memory_space=pltpu.HBM)
    dma = pltpu.SemaphoreType.DMA
    return pl.pallas_call(
        kernel,
        out_shape=(pltpu.VMEM((ROWS, COLS), F32), pltpu.VMEM((2 * NB, COLS), F32)),
        in_specs=[hbm] * 5,
        out_specs=(pl.BlockSpec(memory_space=pltpu.VMEM), pl.BlockSpec(memory_space=pltpu.VMEM)),
        scratch_shapes=[
            pltpu.VMEM((2, NB, ROWS), F32),
            pltpu.VMEM((ROWS, COLS), BF16),
            pltpu.VMEM((ROWS, COLS), BF16),
            pltpu.VMEM((2, ROWS, NB), BF16),
            pltpu.VMEM((2, ROWS, NB), BF16),
            pltpu.VMEM((2, NB, NB), F32),
            pltpu.VMEM((11, 64, COLS), F32),
            pltpu.VMEM((11, NX, 16, COLS), F32),
            pltpu.VMEM((11, NZ, 16, COLS), F32),
            pltpu.VMEM((2, NB, COLS), F32),
            pltpu.VMEM((NB, NB), F32),
            pltpu.VMEM((NB, COLS), F32),
            dma((12,)),
            dma((2, 2, UNITS)), dma((2, 2, UNITS)),
            dma((2, 2, UNITS)), dma((2, 2, UNITS)),
            dma((2, 4, UNITS)), dma((2, 4, UNITS)),
            dma((11, NX - 1)), dma((11, NX - 1)),
            dma((11, NZ - 1)), dma((11, NZ - 1)),
            dma((11, NX - 1)), dma((11, NX - 1)),
            dma((4,)), dma((4,)),
            dma((4,)), dma((4,)),
        ],
        compiler_params=pltpu.CompilerParams(collective_id=0, has_side_effects=True, vmem_limit_bytes=56 << 20),
    )(modes, panel_one.T, panel_two.T, factor_one, factor_two)


def solution(mesh):
    return jax.shard_map(
        shards,
        mesh=mesh,
        in_specs=(P("row", "col"), P("row", "col"), P("row", "col"), P(), P()),
        out_specs=(P("row", "col"), P(None, "col")),
        check_vma=False,
    )
```

```python
import functools

import jax
import jax.numpy as jnp
from jax import lax
from jax.experimental import pallas as pl
from jax.experimental.pallas import tpu as pltpu
from jax.sharding import PartitionSpec as P

MESH = pl.DeviceIdType.MESH
F32, BF16 = jnp.float32, jnp.bfloat16
ROWS, COLS, NB = 4096, 256, 256
SHARE = 32
UNITS, UNIT = 4, 8
HALF = ROWS // 2
NX, NY, NZ = 4, 4, 8
GRAM = 12
STEP, TURN = 2048, 512
PLACE = {0: 0, 1: 1, 3: 2, 2: 3}
AWAY = [0, 1, 3, 2]


def split(value):
    high = value.astype(BF16)
    return high, (value - high.astype(F32)).astype(BF16)


def dot(a, b):
    return jnp.dot(a, b, preferred_element_type=F32)


def triple(a, b):
    ah, al = split(a)
    bh, bl = split(b)
    return dot(ah, bh) + (dot(al, bh) + dot(ah, bl))


def kernel(
    modes, panel_one, panel_two, factor_one, factor_two, work, high_one, low_one, near_one, coords,
    gathered, mode_high, mode_low, high_two, low_two, factors, part, from_x, from_z, sums, gram, right_side,
    load_sem, own_send, own_recv, fwd_send, fwd_recv, sib_send, sib_recv,
    x_send, x_recv, z_send, z_recv, back_send, back_recv, gram_send, gram_recv, gsib_send, gsib_recv,
):
    row, col = lax.axis_index("row"), lax.axis_index("col")
    z, x, y, k = row // NX, row % NX, col // 2, col % 2
    up, down = (row, lax.rem(y + 1, NY) * 2 + k), (row, lax.rem(y + NY - 1, NY) * 2 + k)
    sibling = (row, y * 2 + 1 - k)
    across = (row, lax.rem(y + 2, NY) * 2 + k)
    x_peer = [None] + [(z * NX + lax.rem(x + d, NX), col) for d in range(1, NX)]
    z_peer = [None] + [(lax.rem(z + d, NZ) * NX + x, col) for d in range(1, NZ)]
    panels = (panel_two, panel_one)
    high, low = (high_two, high_one), (low_two, low_one)
    mine = pl.ds(pl.multiple_of(k * SHARE, SHARE), SHARE)
    sends = []

    def remote(src, dst, send, recv, device):
        copy = pltpu.make_async_remote_copy(
            src_ref=src, dst_ref=dst, send_sem=send, recv_sem=recv, device_id=device, device_id_type=MESH
        )
        copy.start()
        sends.append(copy)
        return copy

    loads = []
    for p in range(2):
        loads.append(pltpu.make_async_copy(panels[p], gathered.at[p, mine], load_sem.at[p]))
    for i in range(8):
        rows = pl.ds(i * 512, 512)
        loads.append(pltpu.make_async_copy(modes.at[rows], work.at[rows], load_sem.at[4 + i]))
    loads.append(pltpu.make_async_copy(factor_two, factors.at[0], load_sem.at[2]))
    loads.append(pltpu.make_async_copy(factor_one, factors.at[1], load_sem.at[3]))
    for copy in loads:
        copy.start()

    barrier = pltpu.get_barrier_semaphore()
    friends = [up, down, across, sibling] + x_peer[1:] + z_peer[1:]
    for device in friends:
        pl.semaphore_signal(barrier, inc=1, device_id=device, device_id_type=MESH)
    pl.semaphore_wait(barrier, len(friends))

    def unit_rows(place, u):
        return pl.ds(pl.multiple_of(place * 64 + k * SHARE + u * UNIT, UNIT), UNIT)

    def send_own(p, units, got):
        for u in units:
            src = panels[p].at[pl.ds(u * UNIT, UNIT)]
            for way, (device, away) in enumerate(((up, 3), (down, 1))):
                got[way, u] = remote(
                    src, gathered.at[p, unit_rows(PLACE[away], u)], own_send.at[p, way, u], own_recv.at[p, way, u], device
                )
        return got

    def to_sibling(p, place, u):
        rows = unit_rows(place, u)
        return remote(
            gathered.at[p, rows], gathered.at[p, rows], sib_send.at[p, place, u], sib_recv.at[p, place, u], sibling
        )

    def pass_on(p, own, u):
        copies = []
        for way, (device, away) in enumerate(((up, 3), (down, 1))):
            own[way, u].wait_recv()
            lanes = pl.ds(way * HALF, HALF)
            copies.append(remote(
                gathered.at[p, unit_rows(PLACE[away], u), lanes], gathered.at[p, unit_rows(3, u), lanes],
                fwd_send.at[p, way, u], fwd_recv.at[p, way, u], device,
            ))
        return copies, [to_sibling(p, PLACE[away], u) for away in (3, 1)]

    def multiply(p, slices, group):
        count = sum(n for _, n in slices)

        def step(i, total):
            lanes = pl.ds(pl.multiple_of(i * STEP, STEP), STEP)
            rows = [gathered[p, at:at + n, lanes] for at, n in slices]
            h, l = split(rows[0] if len(rows) == 1 else jnp.concatenate(rows, axis=0))
            two = dot(jnp.concatenate([h, l], axis=0), mode_high[lanes])
            return total + (two[:count] + two[count:] + dot(h, mode_low[lanes]))

        total = lax.fori_loop(0, ROWS // STEP, step, jnp.zeros((count, COLS), F32))
        if isinstance(group, tuple):
            for i, g in enumerate(group):
                part[g, 0:16] = total[i * 16:(i + 1) * 16]
        else:
            part[group, 0:count] = total

    def turn(p, pair):
        @pl.loop(0, ROWS // TURN)
        def _(i):
            lanes = pl.ds(pl.multiple_of(i * TURN, TURN), TURN)
            h, l = split(gathered[p, pair * 128:(pair + 1) * 128, lanes].T)
            high[p][lanes, pair * 128:(pair + 1) * 128] = h
            low[p][lanes, pair * 128:(pair + 1) * 128] = l

    class Group:
        def __init__(self, group, m, target, base):
            self.group, self.m, self.target, self.base = group, m, target, base

        def piece(self, at):
            return pl.ds(pl.multiple_of(at * self.m, self.m), self.m)

        def share_out(self):
            g, m = self.group, self.m
            self.copies = [
                remote(part.at[g, self.piece(lax.rem(x + d, NX))], from_x.at[g, d - 1, pl.ds(0, m)],
                       x_send.at[g, d - 1], x_recv.at[g, d - 1], x_peer[d])
                for d in range(1, NX)
            ]

        def to_z(self, value):
            g, m = self.group, self.m
            from_z[g, z, 0:m] = value
            self.copies = [
                remote(from_z.at[g, z, pl.ds(0, m)], from_z.at[g, z, pl.ds(0, m)],
                       z_send.at[g, d - 1], z_recv.at[g, d - 1], z_peer[d])
                for d in range(1, NZ)
            ]

        def exchange(self):
            g, m = self.group, self.m
            self.finish()
            self.to_z(part[g, self.piece(x)] + from_x[g, 0, 0:m] + from_x[g, 1, 0:m] + from_x[g, 2, 0:m])

        def z_sum(self):
            self.finish()
            total = from_z[self.group, 0, 0:self.m]
            for i in range(1, NZ):
                total += from_z[self.group, i, 0:self.m]
            return total

        def collect(self):
            g = self.group
            rows = pl.ds(pl.multiple_of(self.base, self.m), self.m)
            self.target[rows] = self.z_sum()
            self.copies = [
                remote(self.target.at[rows], self.target.at[rows], back_send.at[g, d - 1], back_recv.at[g, d - 1], x_peer[d])
                for d in range(1, NX)
            ]

        def finish(self):
            for copy in self.copies:
                copy.wait_recv()

    class Ahead(Group):
        def share_out(self):
            self.to_x(part[self.group, 0:self.m])

        def to_x(self, value):
            g, m = self.group, self.m
            from_x[g, x, 0:m] = value
            self.copies = [
                remote(from_x.at[g, x, pl.ds(0, m)], from_x.at[g, x, pl.ds(0, m)], x_send.at[g, d - 1], x_recv.at[g, d - 1], x_peer[d])
                for d in range(1, NX)
            ]

        def x_sum(self):
            self.finish()
            g, m = self.group, self.m
            return ((from_x[g, 0, 0:m] + from_x[g, 1, 0:m]) + from_x[g, 2, 0:m]) + from_x[g, 3, 0:m]

        def exchange(self):
            self.to_z(self.x_sum())

        def collect(self):
            self.store(self.z_sum())

        def store(self, total):
            self.target[pl.ds(pl.multiple_of(self.base, self.m), self.m)] = total

    class Behind(Ahead):
        def share_out(self):
            self.to_z(part[self.group, 0:self.m])

        def exchange(self):
            self.to_x(self.z_sum())

        def collect(self):
            self.store(self.x_sum())

    def block(away):
        return lax.rem(y + away, NY) * 64

    own = [Group(p, 16, sums.at[p], block(0) + x * 16) for p in range(2)]
    near = [
        [Group(2 + 2 * p + h, 16, sums.at[p], block(1 + 2 * (x // 2)) + (x % 2) * SHARE + h * 16) for h in range(2)]
        for p in range(2)
    ]
    far_two = Group(6, 16, sums.at[0], block(2) + x * 16)
    far_one = Group(7, 8, sums.at[1], block(2) + (x // 2) * SHARE + (x % 2) * UNIT)
    tail = [kind(8 + core, 16, sums.at[1], block(2) + core * SHARE + 16) for core, kind in enumerate((Ahead, Behind))]
    gram_group = Group(GRAM, 8, gram, k * SHARE + x * 8)

    def near_rows(h):
        return [(place * 64 + core * SHARE + h * 16, 16) for place in (1, 2) for core in range(2)]

    def local(value, home):
        return jnp.concatenate(
            [value[pl.ds(pl.multiple_of(lax.rem(home + AWAY[s], NY) * 64, 64), 64)] for s in range(4)], axis=0
        )

    own_two = send_own(0, range(UNITS), {})
    sib_own = []
    for p in range(2):
        for u in range(UNITS):
            rows = unit_rows(0, u)
            sib_own.append(remote(
                panels[p].at[pl.ds(u * UNIT, UNIT)], gathered.at[p, rows], sib_send.at[p, 0, u], sib_recv.at[p, 0, u], sibling
            ))
    for copy in loads:
        copy.wait()

    @pl.loop(0, 8)
    def _(i):
        rows = pl.ds(pl.multiple_of(i * 512, 512), 512)
        mode_high[rows], mode_low[rows] = split(work[rows])

    for copy in sib_own:
        copy.wait_recv()
    for p in range(2):
        multiply(p, [(0, 64)], p)
        own[p].share_out()

    def relay(p, sent, u):
        copies, swaps = pass_on(p, sent, u)
        return copies, swaps

    def wait(copies):
        for copy in copies:
            copy.wait_recv()

    def far_unit(p, copies, u):
        wait(copies)
        return to_sibling(p, 3, u)

    def gram_part():
        def step(i, total):
            lanes = pl.ds(pl.multiple_of(i * STEP, STEP), STEP)
            h, l = split(gathered[1, mine, lanes])
            two = dot(jnp.concatenate([h, l], axis=0), high_two[lanes])
            return total + (two[:SHARE] + two[SHARE:] + dot(h, low_two[lanes]))

        part[GRAM, 0:SHARE] = lax.fori_loop(0, ROWS // STEP, step, jnp.zeros((SHARE, NB), F32))

    def update(p, c, chunks):
        ch, cl = split(c)
        @pl.loop(chunks.start, chunks.stop)
        def _(i):
            rows = pl.ds(pl.multiple_of(i * 512, 512), 512)
            h = high[p][rows]
            work[rows] = work[rows] - (dot(h, ch) + dot(low[p][rows], ch) + dot(h, cl))

    on, swaps = [None] * UNITS, [None] * UNITS
    on[0], swaps[0] = relay(0, own_two, 0)
    own[0].exchange()
    own[1].exchange()
    on[1], swaps[1] = relay(0, own_two, 1)
    wait(swaps[0] + swaps[1])
    multiply(0, near_rows(0), near[0][0].group)
    near[0][0].share_out()
    on[2], swaps[2] = relay(0, own_two, 2)
    on[3], swaps[3] = relay(0, own_two, 3)
    own_one = send_own(1, range(UNITS), {})
    near[0][0].exchange()
    wait(swaps[2] + swaps[3])
    multiply(0, near_rows(1), near[0][1].group)
    near[0][1].share_out()
    own[0].collect()
    own[1].collect()
    turn(0, 0)
    far = [far_unit(0, on[u], u) for u in range(UNITS)]
    near[0][1].exchange()
    wait(far)
    multiply(0, [(192, 64)], far_two.group)
    far_two.share_out()
    turn(0, 1)
    on[0], swaps[0] = relay(1, own_one, 0)
    gram_part()
    gram_group.share_out()
    near[0][0].collect()
    on[1], swaps[1] = relay(1, own_one, 1)
    far_two.exchange()
    wait(swaps[0] + swaps[1])
    multiply(1, near_rows(0), near[1][0].group)
    near[1][0].share_out()
    near[0][1].collect()
    on[2], swaps[2] = relay(1, own_one, 2)
    gram_group.exchange()
    on[3], swaps[3] = relay(1, own_one, 3)
    near[1][0].exchange()
    wait(swaps[2] + swaps[3])
    multiply(1, near_rows(1), near[1][1].group)
    near[1][1].share_out()
    far = [far_unit(1, on[u], u) for u in range(2)]
    far_two.collect()
    gram_group.collect()
    wait(far)
    multiply(1, [(192, 16), (224, 16)], far_one.group)
    far_one.share_out()
    far = [far_unit(1, on[2], 2)]
    near[1][1].exchange()
    far.append(far_unit(1, on[3], 3))
    wait(far)
    multiply(1, [(208, 16), (240, 16)], (8, 9))
    tail[1].share_out()
    tail[0].share_out()
    near[1][0].collect()
    far_one.exchange()
    gram_group.finish()
    around = [
        remote(gram.at[mine], gram.at[pl.ds(pl.multiple_of(away * 64 + k * SHARE, SHARE), SHARE)],
               gram_send.at[away], gram_recv.at[away], device)
        for away, device in ((3, up), (1, down), (2, across))
    ]
    for group in (own[0], near[0][0], near[0][1], far_two):
        group.finish()
    coords[NB:2 * NB] = triple(factors[0], sums[0])
    two_at = coords.at[NB:2 * NB]
    near_two = local(two_at, y)
    turn(1, 0)
    tail[0].exchange()
    update(0, near_two, range(0, 3))
    near[1][1].collect()
    wait(around)
    swap = []
    for away in range(4):
        rows = pl.ds(pl.multiple_of(away * 64 + k * SHARE, SHARE), SHARE)
        swap.append(remote(gram.at[rows], gram.at[rows], gsib_send.at[away], gsib_recv.at[away], sibling))
    tail[1].exchange()
    far_one.collect()
    update(0, near_two, range(3, 8))
    turn(1, 1)
    wait(swap)
    for away in range(4):
        home = lax.rem(y + away, NY)
        right_side[pl.ds(pl.multiple_of(home * 64, 64), 64)] = triple(gram[away * 64:(away + 1) * 64], local(two_at, home))
    for group in (own[1], near[1][0], near[1][1], far_one):
        group.finish()
    for group in tail:
        group.collect()
    coords[0:NB] = triple(factors[1], sums[1] - right_side[...])
    near_one[...] = local(coords.at[0:NB], y)
    for copy in sends:
        copy.wait_send()


CHUNKS = 8


def last_update(work, high, low, near_one, coords, updated, coords_out, stage, sem):
    copies = [pltpu.make_async_copy(coords, coords_out, sem.at[CHUNKS])]
    copies[0].start()
    ch, cl = split(near_one[...])
    size = ROWS // CHUNKS
    for i in range(CHUNKS):
        rows = slice(i * size, (i + 1) * size)
        h = high[rows]
        stage[rows] = work[rows] - (dot(h, ch) + dot(low[rows], ch) + dot(h, cl))
        copies.append(pltpu.make_async_copy(stage.at[rows], updated.at[rows], sem.at[i]))
        copies[-1].start()
    for copy in copies:
        copy.wait()


def shards(modes, panel_one, panel_two, factor_one, factor_two):
    hbm, vmem = pl.BlockSpec(memory_space=pltpu.HBM), pl.BlockSpec(memory_space=pltpu.VMEM)
    dma = pltpu.SemaphoreType.DMA
    state = pl.pallas_call(
        kernel,
        out_shape=(
            pltpu.VMEM((ROWS, COLS), F32), pltpu.VMEM((ROWS, NB), BF16), pltpu.VMEM((ROWS, NB), BF16),
            pltpu.VMEM((NB, COLS), F32), pltpu.VMEM((2 * NB, COLS), F32),
        ),
        in_specs=[hbm] * 5,
        out_specs=(vmem,) * 5,
        scratch_shapes=[
            pltpu.VMEM((2, NB, ROWS), F32),
            pltpu.VMEM((ROWS, COLS), BF16),
            pltpu.VMEM((ROWS, COLS), BF16),
            pltpu.VMEM((ROWS, NB), BF16),
            pltpu.VMEM((ROWS, NB), BF16),
            pltpu.VMEM((2, NB, NB), F32),
            pltpu.VMEM((13, 64, COLS), F32),
            pltpu.VMEM((13, NX, 16, COLS), F32),
            pltpu.VMEM((13, NZ, 16, COLS), F32),
            pltpu.VMEM((2, NB, COLS), F32),
            pltpu.VMEM((NB, NB), F32),
            pltpu.VMEM((NB, COLS), F32),
            dma((12,)),
            dma((2, 2, UNITS)), dma((2, 2, UNITS)),
            dma((2, 2, UNITS)), dma((2, 2, UNITS)),
            dma((2, 4, UNITS)), dma((2, 4, UNITS)),
            dma((13, NX - 1)), dma((13, NX - 1)),
            dma((13, NZ - 1)), dma((13, NZ - 1)),
            dma((13, NX - 1)), dma((13, NX - 1)),
            dma((4,)), dma((4,)),
            dma((4,)), dma((4,)),
        ],
        compiler_params=pltpu.CompilerParams(collective_id=0, has_side_effects=True, vmem_limit_bytes=54 << 20),
    )(modes, panel_one.T, panel_two.T, factor_one, factor_two)
    return pl.pallas_call(
        last_update,
        out_shape=(jax.ShapeDtypeStruct((ROWS, COLS), F32), jax.ShapeDtypeStruct((2 * NB, COLS), F32)),
        in_specs=[vmem] * 5,
        out_specs=(hbm, hbm),
        scratch_shapes=[pltpu.VMEM((ROWS, COLS), F32), dma((CHUNKS + 1,))],
        compiler_params=pltpu.CompilerParams(vmem_limit_bytes=24 << 20),
    )(*state)


def solution(mesh):
    return jax.shard_map(
        shards,
        mesh=mesh,
        in_specs=(P("row", "col"), P("row", "col"), P("row", "col"), P(), P()),
        out_specs=(P("row", "col"), P(None, "col")),
        check_vma=False,
    )
```

```python
import functools

import jax
import jax.numpy as jnp
from jax import lax
from jax.experimental import pallas as pl
from jax.experimental.pallas import tpu as pltpu
from jax.sharding import PartitionSpec as P

MESH = pl.DeviceIdType.MESH
F32, BF16 = jnp.float32, jnp.bfloat16
ROWS, COLS, NB = 4096, 256, 256
SHARE = 32
UNITS, UNIT = 4, 8
HALF = ROWS // 2
NX, NY, NZ = 4, 4, 8
GRAM = 12
STEP, TURN = 2048, 512
PLACE = {0: 0, 1: 1, 3: 2, 2: 3}
AWAY = [0, 1, 3, 2]


def split(value):
    high = value.astype(BF16)
    return high, (value - high.astype(F32)).astype(BF16)


def dot(a, b):
    return jnp.dot(a, b, preferred_element_type=F32)


def triple(a, b):
    ah, al = split(a)
    bh, bl = split(b)
    return dot(ah, bh) + (dot(al, bh) + dot(ah, bl))


def kernel(
    modes, panel_one, panel_two, factor_one, factor_two, work, high_one, low_one, near_one, coords,
    gathered, mode_high, mode_low, high_two, low_two, factors, part, from_x, from_z, sums, gram, right_side,
    load_sem, own_send, own_recv, fwd_send, fwd_recv, sib_send, sib_recv,
    x_send, x_recv, z_send, z_recv, back_send, back_recv, gram_send, gram_recv, gsib_send, gsib_recv,
):
    row, col = lax.axis_index("row"), lax.axis_index("col")
    z, x, y, k = row // NX, row % NX, col // 2, col % 2
    up, down = (row, lax.rem(y + 1, NY) * 2 + k), (row, lax.rem(y + NY - 1, NY) * 2 + k)
    sibling = (row, y * 2 + 1 - k)
    across = (row, lax.rem(y + 2, NY) * 2 + k)
    x_peer = [None] + [(z * NX + lax.rem(x + d, NX), col) for d in range(1, NX)]
    z_peer = [None] + [(lax.rem(z + d, NZ) * NX + x, col) for d in range(1, NZ)]
    panels = (panel_two, panel_one)
    high, low = (high_two, high_one), (low_two, low_one)
    mine = pl.ds(pl.multiple_of(k * SHARE, SHARE), SHARE)
    sends = []

    def remote(src, dst, send, recv, device):
        copy = pltpu.make_async_remote_copy(
            src_ref=src, dst_ref=dst, send_sem=send, recv_sem=recv, device_id=device, device_id_type=MESH
        )
        copy.start()
        sends.append(copy)
        return copy

    loads = []
    for p in range(2):
        loads.append(pltpu.make_async_copy(panels[p], gathered.at[p, mine], load_sem.at[p]))
    for i in range(8):
        rows = pl.ds(i * 512, 512)
        loads.append(pltpu.make_async_copy(modes.at[rows], work.at[rows], load_sem.at[4 + i]))
    loads.append(pltpu.make_async_copy(factor_two, factors.at[0], load_sem.at[2]))
    loads.append(pltpu.make_async_copy(factor_one, factors.at[1], load_sem.at[3]))
    for copy in loads:
        copy.start()

    barrier = pltpu.get_barrier_semaphore()
    friends = [up, down, across, sibling] + x_peer[1:] + z_peer[1:]
    for device in friends:
        pl.semaphore_signal(barrier, inc=1, device_id=device, device_id_type=MESH)
    pl.semaphore_wait(barrier, len(friends))

    def unit_rows(place, u):
        return pl.ds(pl.multiple_of(place * 64 + k * SHARE + u * UNIT, UNIT), UNIT)

    def send_own(p, units, got):
        for u in units:
            src = panels[p].at[pl.ds(u * UNIT, UNIT)]
            for way, (device, away) in enumerate(((up, 3), (down, 1))):
                got[way, u] = remote(
                    src, gathered.at[p, unit_rows(PLACE[away], u)], own_send.at[p, way, u], own_recv.at[p, way, u], device
                )
        return got

    def to_sibling(p, place, u):
        rows = unit_rows(place, u)
        return remote(
            gathered.at[p, rows], gathered.at[p, rows], sib_send.at[p, place, u], sib_recv.at[p, place, u], sibling
        )

    def pass_on(p, own, u):
        copies = []
        for way, (device, away) in enumerate(((up, 3), (down, 1))):
            own[way, u].wait_recv()
            lanes = pl.ds(way * HALF, HALF)
            copies.append(remote(
                gathered.at[p, unit_rows(PLACE[away], u), lanes], gathered.at[p, unit_rows(3, u), lanes],
                fwd_send.at[p, way, u], fwd_recv.at[p, way, u], device,
            ))
        return copies, [to_sibling(p, PLACE[away], u) for away in (3, 1)]

    def multiply(p, slices, group):
        count = sum(n for _, n in slices)

        def step(i, total):
            lanes = pl.ds(pl.multiple_of(i * STEP, STEP), STEP)
            rows = [gathered[p, at:at + n, lanes] for at, n in slices]
            h, l = split(rows[0] if len(rows) == 1 else jnp.concatenate(rows, axis=0))
            two = dot(jnp.concatenate([h, l], axis=0), mode_high[lanes])
            return total + (two[:count] + two[count:] + dot(h, mode_low[lanes]))

        total = lax.fori_loop(0, ROWS // STEP, step, jnp.zeros((count, COLS), F32))
        part[group, 0:count] = total

    def turn(p, pair):
        @pl.loop(0, ROWS // TURN)
        def _(i):
            lanes = pl.ds(pl.multiple_of(i * TURN, TURN), TURN)
            h, l = split(gathered[p, pair * 128:(pair + 1) * 128, lanes].T)
            high[p][lanes, pair * 128:(pair + 1) * 128] = h
            low[p][lanes, pair * 128:(pair + 1) * 128] = l

    class Group:
        def __init__(self, group, m, target, base):
            self.group, self.m, self.target, self.base = group, m, target, base

        def piece(self, at):
            return pl.ds(pl.multiple_of(at * self.m, self.m), self.m)

        def share_out(self):
            g, m = self.group, self.m
            self.copies = [
                remote(part.at[g, self.piece(lax.rem(x + d, NX))], from_x.at[g, d - 1, pl.ds(0, m)],
                       x_send.at[g, d - 1], x_recv.at[g, d - 1], x_peer[d])
                for d in range(1, NX)
            ]

        def to_z(self, value):
            g, m = self.group, self.m
            from_z[g, z, 0:m] = value
            self.copies = [
                remote(from_z.at[g, z, pl.ds(0, m)], from_z.at[g, z, pl.ds(0, m)],
                       z_send.at[g, d - 1], z_recv.at[g, d - 1], z_peer[d])
                for d in range(1, NZ)
            ]

        def exchange(self):
            g, m = self.group, self.m
            self.finish()
            self.to_z(part[g, self.piece(x)] + from_x[g, 0, 0:m] + from_x[g, 1, 0:m] + from_x[g, 2, 0:m])

        def z_sum(self):
            self.finish()
            total = from_z[self.group, 0, 0:self.m]
            for i in range(1, NZ):
                total += from_z[self.group, i, 0:self.m]
            return total

        def collect(self):
            g = self.group
            rows = pl.ds(pl.multiple_of(self.base, self.m), self.m)
            self.target[rows] = self.z_sum()
            self.copies = [
                remote(self.target.at[rows], self.target.at[rows], back_send.at[g, d - 1], back_recv.at[g, d - 1], x_peer[d])
                for d in range(1, NX)
            ]

        def finish(self):
            for copy in self.copies:
                copy.wait_recv()

    def block(away):
        return lax.rem(y + away, NY) * 64

    own = [Group(p, 16, sums.at[p], block(0) + x * 16) for p in range(2)]
    near = [
        [Group(2 + 2 * p + h, 16, sums.at[p], block(1 + 2 * (x // 2)) + (x % 2) * SHARE + h * 16) for h in range(2)]
        for p in range(2)
    ]
    far_two = Group(6, 16, sums.at[0], block(2) + x * 16)
    far_one = Group(7, 8, sums.at[1], block(2) + (x // 2) * SHARE + (x % 2) * UNIT)
    tail = Group(8, 8, sums.at[1], block(2) + (x // 2) * SHARE + 16 + (x % 2) * UNIT)
    gram_group = Group(GRAM, 8, gram, k * SHARE + x * 8)

    def near_rows(h):
        return [(place * 64 + core * SHARE + h * 16, 16) for place in (1, 2) for core in range(2)]

    def local(value, home):
        return jnp.concatenate(
            [value[pl.ds(pl.multiple_of(lax.rem(home + AWAY[s], NY) * 64, 64), 64)] for s in range(4)], axis=0
        )

    own_two = send_own(0, range(UNITS), {})
    sib_own = []
    for p in range(2):
        for u in range(UNITS):
            rows = unit_rows(0, u)
            sib_own.append(remote(
                panels[p].at[pl.ds(u * UNIT, UNIT)], gathered.at[p, rows], sib_send.at[p, 0, u], sib_recv.at[p, 0, u], sibling
            ))
    for copy in loads:
        copy.wait()

    @pl.loop(0, 8)
    def _(i):
        rows = pl.ds(pl.multiple_of(i * 512, 512), 512)
        mode_high[rows], mode_low[rows] = split(work[rows])

    for copy in sib_own:
        copy.wait_recv()
    for p in range(2):
        multiply(p, [(0, 64)], p)
        own[p].share_out()

    def relay(p, sent, u):
        copies, swaps = pass_on(p, sent, u)
        return copies, swaps

    def wait(copies):
        for copy in copies:
            copy.wait_recv()

    def far_unit(p, copies, u):
        wait(copies)
        return to_sibling(p, 3, u)

    def gram_part():
        def step(i, total):
            lanes = pl.ds(pl.multiple_of(i * STEP, STEP), STEP)
            h, l = split(gathered[1, mine, lanes])
            two = dot(jnp.concatenate([h, l], axis=0), high_two[lanes])
            return total + (two[:SHARE] + two[SHARE:] + dot(h, low_two[lanes]))

        part[GRAM, 0:SHARE] = lax.fori_loop(0, ROWS // STEP, step, jnp.zeros((SHARE, NB), F32))

    def update(p, c, chunks):
        ch, cl = split(c)
        @pl.loop(chunks.start, chunks.stop)
        def _(i):
            rows = pl.ds(pl.multiple_of(i * 512, 512), 512)
            h = high[p][rows]
            work[rows] = work[rows] - (dot(h, ch) + dot(low[p][rows], ch) + dot(h, cl))

    on, swaps = [None] * UNITS, [None] * UNITS
    on[0], swaps[0] = relay(0, own_two, 0)
    own[0].exchange()
    own[1].exchange()
    on[1], swaps[1] = relay(0, own_two, 1)
    wait(swaps[0] + swaps[1])
    multiply(0, near_rows(0), near[0][0].group)
    near[0][0].share_out()
    on[2], swaps[2] = relay(0, own_two, 2)
    on[3], swaps[3] = relay(0, own_two, 3)
    own_one = send_own(1, range(UNITS), {})
    near[0][0].exchange()
    wait(swaps[2] + swaps[3])
    multiply(0, near_rows(1), near[0][1].group)
    near[0][1].share_out()
    own[0].collect()
    own[1].collect()
    turn(0, 0)
    far = [far_unit(0, on[u], u) for u in range(UNITS)]
    near[0][1].exchange()
    wait(far)
    multiply(0, [(192, 64)], far_two.group)
    far_two.share_out()
    turn(0, 1)
    on[0], swaps[0] = relay(1, own_one, 0)
    gram_part()
    gram_group.share_out()
    near[0][0].collect()
    on[1], swaps[1] = relay(1, own_one, 1)
    far_two.exchange()
    wait(swaps[0] + swaps[1])
    multiply(1, near_rows(0), near[1][0].group)
    near[1][0].share_out()
    near[0][1].collect()
    on[2], swaps[2] = relay(1, own_one, 2)
    gram_group.exchange()
    on[3], swaps[3] = relay(1, own_one, 3)
    near[1][0].exchange()
    wait(swaps[2] + swaps[3])
    multiply(1, near_rows(1), near[1][1].group)
    near[1][1].share_out()
    far_two.collect()
    far = [far_unit(1, on[u], u) for u in range(2)]
    gram_group.collect()
    wait(far)
    multiply(1, [(192, 16), (224, 16)], far_one.group)
    far_one.share_out()
    far = [far_unit(1, on[2], 2)]
    near[1][1].exchange()
    far.append(far_unit(1, on[3], 3))
    for group in (own[0], near[0][0], near[0][1], far_two):
        group.finish()
    coords[NB:2 * NB] = triple(factors[0], sums[0])
    wait(far)
    multiply(1, [(208, 16), (240, 16)], 8)
    tail.share_out()
    near[1][0].collect()
    far_one.exchange()
    gram_group.finish()
    around = [
        remote(gram.at[mine], gram.at[pl.ds(pl.multiple_of(away * 64 + k * SHARE, SHARE), SHARE)],
               gram_send.at[away], gram_recv.at[away], device)
        for away, device in ((3, up), (1, down), (2, across))
    ]
    two_at = coords.at[NB:2 * NB]
    near_two = local(two_at, y)
    turn(1, 0)
    tail.exchange()
    update(0, near_two, range(0, 3))
    near[1][1].collect()
    wait(around)
    swap = []
    for away in range(4):
        rows = pl.ds(pl.multiple_of(away * 64 + k * SHARE, SHARE), SHARE)
        swap.append(remote(gram.at[rows], gram.at[rows], gsib_send.at[away], gsib_recv.at[away], sibling))
    far_one.collect()
    update(0, near_two, range(3, 8))
    wait(swap)
    for away in range(4):
        home = lax.rem(y + away, NY)
        right_side[pl.ds(pl.multiple_of(home * 64, 64), 64)] = triple(gram[away * 64:(away + 1) * 64], local(two_at, home))
    tail.collect()
    turn(1, 1)
    for group in (own[1], near[1][0], near[1][1], far_one, tail):
        group.finish()
    coords[0:NB] = triple(factors[1], sums[1] - right_side[...])
    near_one[...] = local(coords.at[0:NB], y)
    for copy in sends:
        copy.wait_send()


CHUNKS = 8


def last_update(work, high, low, near_one, coords, updated, coords_out, stage, sem):
    copies = [pltpu.make_async_copy(coords, coords_out, sem.at[CHUNKS])]
    copies[0].start()
    ch, cl = split(near_one[...])
    size = ROWS // CHUNKS
    for i in range(CHUNKS):
        rows = slice(i * size, (i + 1) * size)
        h = high[rows]
        stage[rows] = work[rows] - (dot(h, ch) + dot(low[rows], ch) + dot(h, cl))
        copies.append(pltpu.make_async_copy(stage.at[rows], updated.at[rows], sem.at[i]))
        copies[-1].start()
    for copy in copies:
        copy.wait()


def shards(modes, panel_one, panel_two, factor_one, factor_two):
    hbm, vmem = pl.BlockSpec(memory_space=pltpu.HBM), pl.BlockSpec(memory_space=pltpu.VMEM)
    dma = pltpu.SemaphoreType.DMA
    state = pl.pallas_call(
        kernel,
        out_shape=(
            pltpu.VMEM((ROWS, COLS), F32), pltpu.VMEM((ROWS, NB), BF16), pltpu.VMEM((ROWS, NB), BF16),
            pltpu.VMEM((NB, COLS), F32), pltpu.VMEM((2 * NB, COLS), F32),
        ),
        in_specs=[hbm] * 5,
        out_specs=(vmem,) * 5,
        scratch_shapes=[
            pltpu.VMEM((2, NB, ROWS), F32),
            pltpu.VMEM((ROWS, COLS), BF16),
            pltpu.VMEM((ROWS, COLS), BF16),
            pltpu.VMEM((ROWS, NB), BF16),
            pltpu.VMEM((ROWS, NB), BF16),
            pltpu.VMEM((2, NB, NB), F32),
            pltpu.VMEM((13, 64, COLS), F32),
            pltpu.VMEM((13, NX, 16, COLS), F32),
            pltpu.VMEM((13, NZ, 16, COLS), F32),
            pltpu.VMEM((2, NB, COLS), F32),
            pltpu.VMEM((NB, NB), F32),
            pltpu.VMEM((NB, COLS), F32),
            dma((12,)),
            dma((2, 2, UNITS)), dma((2, 2, UNITS)),
            dma((2, 2, UNITS)), dma((2, 2, UNITS)),
            dma((2, 4, UNITS)), dma((2, 4, UNITS)),
            dma((13, NX - 1)), dma((13, NX - 1)),
            dma((13, NZ - 1)), dma((13, NZ - 1)),
            dma((13, NX - 1)), dma((13, NX - 1)),
            dma((4,)), dma((4,)),
            dma((4,)), dma((4,)),
        ],
        compiler_params=pltpu.CompilerParams(collective_id=0, has_side_effects=True, vmem_limit_bytes=54 << 20),
    )(modes, panel_one.T, panel_two.T, factor_one, factor_two)
    return pl.pallas_call(
        last_update,
        out_shape=(jax.ShapeDtypeStruct((ROWS, COLS), F32), jax.ShapeDtypeStruct((2 * NB, COLS), F32)),
        in_specs=[vmem] * 5,
        out_specs=(hbm, hbm),
        scratch_shapes=[pltpu.VMEM((ROWS, COLS), F32), dma((CHUNKS + 1,))],
        compiler_params=pltpu.CompilerParams(vmem_limit_bytes=24 << 20),
    )(*state)


def solution(mesh):
    return jax.shard_map(
        shards,
        mesh=mesh,
        in_specs=(P("row", "col"), P("row", "col"), P("row", "col"), P(), P()),
        out_specs=(P("row", "col"), P(None, "col")),
        check_vma=False,
    )
```

```python
import functools

import jax
import jax.numpy as jnp
from jax import lax
from jax.experimental import pallas as pl
from jax.experimental.pallas import tpu as pltpu
from jax.sharding import PartitionSpec as P

MESH = pl.DeviceIdType.MESH
F32, BF16 = jnp.float32, jnp.bfloat16
ROWS, COLS, NB = 4096, 256, 256
SHARE = 32
UNITS, UNIT = 4, 8
HALF = ROWS // 2
NX, NY, NZ = 4, 4, 8
GRAM = 12
STEP, TURN = 2048, 512
PLACE = {0: 0, 1: 1, 3: 2, 2: 3}
AWAY = [0, 1, 3, 2]


def split(value):
    high = value.astype(BF16)
    return high, (value - high.astype(F32)).astype(BF16)


def dot(a, b):
    return jnp.dot(a, b, preferred_element_type=F32)


def triple(a, b):
    ah, al = split(a)
    bh, bl = split(b)
    return dot(ah, bh) + (dot(al, bh) + dot(ah, bl))


def kernel(
    modes, panel_one, panel_two, factor_one, factor_two, work, high_one, low_one, near_one, coords,
    gathered, mode_high, mode_low, high_two, low_two, factors, part, from_x, from_z, sums, gram, right_side,
    load_sem, own_send, own_recv, fwd_send, fwd_recv, sib_send, sib_recv,
    x_send, x_recv, z_send, z_recv, back_send, back_recv, gram_send, gram_recv, gsib_send, gsib_recv,
):
    row, col = lax.axis_index("row"), lax.axis_index("col")
    z, x, y, k = row // NX, row % NX, col // 2, col % 2
    up, down = (row, lax.rem(y + 1, NY) * 2 + k), (row, lax.rem(y + NY - 1, NY) * 2 + k)
    sibling = (row, y * 2 + 1 - k)
    across = (row, lax.rem(y + 2, NY) * 2 + k)
    x_peer = [None] + [(z * NX + lax.rem(x + d, NX), col) for d in range(1, NX)]
    z_peer = [None] + [(lax.rem(z + d, NZ) * NX + x, col) for d in range(1, NZ)]
    panels = (panel_two, panel_one)
    high, low = (high_two, high_one), (low_two, low_one)
    mine = pl.ds(pl.multiple_of(k * SHARE, SHARE), SHARE)
    sends = []

    def remote(src, dst, send, recv, device):
        copy = pltpu.make_async_remote_copy(
            src_ref=src, dst_ref=dst, send_sem=send, recv_sem=recv, device_id=device, device_id_type=MESH
        )
        copy.start()
        sends.append(copy)
        return copy

    loads = []
    for p in range(2):
        loads.append(pltpu.make_async_copy(panels[p], gathered.at[p, mine], load_sem.at[p]))
    for i in range(8):
        rows = pl.ds(i * 512, 512)
        loads.append(pltpu.make_async_copy(modes.at[rows], work.at[rows], load_sem.at[4 + i]))
    loads.append(pltpu.make_async_copy(factor_two, factors.at[0], load_sem.at[2]))
    loads.append(pltpu.make_async_copy(factor_one, factors.at[1], load_sem.at[3]))
    for copy in loads:
        copy.start()

    barrier = pltpu.get_barrier_semaphore()
    friends = [up, down, across, sibling] + x_peer[1:] + z_peer[1:]
    for device in friends:
        pl.semaphore_signal(barrier, inc=1, device_id=device, device_id_type=MESH)
    pl.semaphore_wait(barrier, len(friends))

    def unit_rows(place, u):
        return pl.ds(pl.multiple_of(place * 64 + k * SHARE + u * UNIT, UNIT), UNIT)

    def send_own(p, units, got):
        for u in units:
            src = panels[p].at[pl.ds(u * UNIT, UNIT)]
            for way, (device, away) in enumerate(((up, 3), (down, 1))):
                got[way, u] = remote(
                    src, gathered.at[p, unit_rows(PLACE[away], u)], own_send.at[p, way, u], own_recv.at[p, way, u], device
                )
        return got

    def to_sibling(p, place, u):
        rows = unit_rows(place, u)
        return remote(
            gathered.at[p, rows], gathered.at[p, rows], sib_send.at[p, place, u], sib_recv.at[p, place, u], sibling
        )

    def pass_on(p, own, u):
        copies = []
        for way, (device, away) in enumerate(((up, 3), (down, 1))):
            own[way, u].wait_recv()
            lanes = pl.ds(way * HALF, HALF)
            copies.append(remote(
                gathered.at[p, unit_rows(PLACE[away], u), lanes], gathered.at[p, unit_rows(3, u), lanes],
                fwd_send.at[p, way, u], fwd_recv.at[p, way, u], device,
            ))
        return copies, [to_sibling(p, PLACE[away], u) for away in (3, 1)]

    def multiply(p, slices, group):
        count = sum(n for _, n in slices)

        def step(i, total):
            lanes = pl.ds(pl.multiple_of(i * STEP, STEP), STEP)
            rows = [gathered[p, at:at + n, lanes] for at, n in slices]
            h, l = split(rows[0] if len(rows) == 1 else jnp.concatenate(rows, axis=0))
            two = dot(jnp.concatenate([h, l], axis=0), mode_high[lanes])
            return total + (two[:count] + two[count:] + dot(h, mode_low[lanes]))

        total = lax.fori_loop(0, ROWS // STEP, step, jnp.zeros((count, COLS), F32))
        part[group, 0:count] = total

    def turn(p, pair):
        @pl.loop(0, ROWS // TURN)
        def _(i):
            lanes = pl.ds(pl.multiple_of(i * TURN, TURN), TURN)
            h, l = split(gathered[p, pair * 128:(pair + 1) * 128, lanes].T)
            high[p][lanes, pair * 128:(pair + 1) * 128] = h
            low[p][lanes, pair * 128:(pair + 1) * 128] = l

    class Group:
        def __init__(self, group, m, target, base):
            self.group, self.m, self.target, self.base = group, m, target, base

        def piece(self, at):
            return pl.ds(pl.multiple_of(at * self.m, self.m), self.m)

        def share_out(self):
            g, m = self.group, self.m
            self.copies = [
                remote(part.at[g, self.piece(lax.rem(x + d, NX))], from_x.at[g, d - 1, pl.ds(0, m)],
                       x_send.at[g, d - 1], x_recv.at[g, d - 1], x_peer[d])
                for d in range(1, NX)
            ]

        def to_z(self, value):
            g, m = self.group, self.m
            from_z[g, z, 0:m] = value
            self.copies = [
                remote(from_z.at[g, z, pl.ds(0, m)], from_z.at[g, z, pl.ds(0, m)],
                       z_send.at[g, d - 1], z_recv.at[g, d - 1], z_peer[d])
                for d in range(1, NZ)
            ]

        def exchange(self):
            g, m = self.group, self.m
            self.finish()
            self.to_z(part[g, self.piece(x)] + from_x[g, 0, 0:m] + from_x[g, 1, 0:m] + from_x[g, 2, 0:m])

        def z_sum(self):
            self.finish()
            total = from_z[self.group, 0, 0:self.m]
            for i in range(1, NZ):
                total += from_z[self.group, i, 0:self.m]
            return total

        def collect(self):
            g = self.group
            rows = pl.ds(pl.multiple_of(self.base, self.m), self.m)
            self.target[rows] = self.z_sum()
            self.copies = [
                remote(self.target.at[rows], self.target.at[rows], back_send.at[g, d - 1], back_recv.at[g, d - 1], x_peer[d])
                for d in range(1, NX)
            ]

        def finish(self):
            for copy in self.copies:
                copy.wait_recv()

    def block(away):
        return lax.rem(y + away, NY) * 64

    own = [Group(p, 16, sums.at[p], block(0) + x * 16) for p in range(2)]
    near = [
        [Group(2 + 2 * p + h, 16, sums.at[p], block(1 + 2 * (x // 2)) + (x % 2) * SHARE + h * 16) for h in range(2)]
        for p in range(2)
    ]
    far_two = Group(6, 16, sums.at[0], block(2) + x * 16)
    far_one = Group(7, 8, sums.at[1], block(2) + (x // 2) * SHARE + (x % 2) * UNIT)
    tail = Group(8, 8, sums.at[1], block(2) + (x // 2) * SHARE + 16 + (x % 2) * UNIT)
    gram_group = Group(GRAM, 8, gram, k * SHARE + x * 8)

    def near_rows(h):
        return [(place * 64 + core * SHARE + h * 16, 16) for place in (1, 2) for core in range(2)]

    def local(value, home):
        return jnp.concatenate(
            [value[pl.ds(pl.multiple_of(lax.rem(home + AWAY[s], NY) * 64, 64), 64)] for s in range(4)], axis=0
        )

    own_two = send_own(0, range(UNITS), {})
    sib_own = []
    for p in range(2):
        for u in range(UNITS):
            rows = unit_rows(0, u)
            sib_own.append(remote(
                panels[p].at[pl.ds(u * UNIT, UNIT)], gathered.at[p, rows], sib_send.at[p, 0, u], sib_recv.at[p, 0, u], sibling
            ))
    for copy in loads:
        copy.wait()

    @pl.loop(0, 8)
    def _(i):
        rows = pl.ds(pl.multiple_of(i * 512, 512), 512)
        mode_high[rows], mode_low[rows] = split(work[rows])

    for copy in sib_own:
        copy.wait_recv()
    for p in range(2):
        multiply(p, [(0, 64)], p)
        own[p].share_out()

    def relay(p, sent, u):
        copies, swaps = pass_on(p, sent, u)
        return copies, swaps

    def wait(copies):
        for copy in copies:
            copy.wait_recv()

    def far_unit(p, copies, u):
        wait(copies)
        return to_sibling(p, 3, u)

    def gram_part():
        def step(i, total):
            lanes = pl.ds(pl.multiple_of(i * STEP, STEP), STEP)
            h, l = split(gathered[1, mine, lanes])
            two = dot(jnp.concatenate([h, l], axis=0), high_two[lanes])
            return total + (two[:SHARE] + two[SHARE:] + dot(h, low_two[lanes]))

        part[GRAM, 0:SHARE] = lax.fori_loop(0, ROWS // STEP, step, jnp.zeros((SHARE, NB), F32))

    def update(p, c, chunks):
        ch, cl = split(c)
        @pl.loop(chunks.start, chunks.stop)
        def _(i):
            rows = pl.ds(pl.multiple_of(i * 512, 512), 512)
            h = high[p][rows]
            work[rows] = work[rows] - (dot(h, ch) + dot(low[p][rows], ch) + dot(h, cl))

    on, swaps = [None] * UNITS, [None] * UNITS
    on[0], swaps[0] = relay(0, own_two, 0)
    own[0].exchange()
    own[1].exchange()
    on[1], swaps[1] = relay(0, own_two, 1)
    wait(swaps[0] + swaps[1])
    multiply(0, near_rows(0), near[0][0].group)
    near[0][0].share_out()
    on[2], swaps[2] = relay(0, own_two, 2)
    on[3], swaps[3] = relay(0, own_two, 3)
    own_one = send_own(1, range(UNITS), {})
    near[0][0].exchange()
    wait(swaps[2] + swaps[3])
    multiply(0, near_rows(1), near[0][1].group)
    near[0][1].share_out()
    own[0].collect()
    own[1].collect()
    turn(0, 0)
    far = [far_unit(0, on[u], u) for u in range(UNITS)]
    near[0][1].exchange()
    wait(far)
    multiply(0, [(192, 64)], far_two.group)
    far_two.share_out()
    turn(0, 1)
    on[0], swaps[0] = relay(1, own_one, 0)
    gram_part()
    gram_group.share_out()
    near[0][0].collect()
    on[1], swaps[1] = relay(1, own_one, 1)
    far_two.exchange()
    wait(swaps[0] + swaps[1])
    multiply(1, near_rows(0), near[1][0].group)
    near[1][0].share_out()
    near[0][1].collect()
    on[2], swaps[2] = relay(1, own_one, 2)
    gram_group.exchange()
    on[3], swaps[3] = relay(1, own_one, 3)
    near[1][0].exchange()
    wait(swaps[2] + swaps[3])
    multiply(1, near_rows(1), near[1][1].group)
    near[1][1].share_out()
    far_two.collect()
    far = [far_unit(1, on[u], u) for u in range(2)]
    gram_group.collect()
    wait(far)
    multiply(1, [(192, 16), (224, 16)], far_one.group)
    far_one.share_out()
    near[1][1].exchange()
    far = [far_unit(1, on[2], 2)]
    far.append(far_unit(1, on[3], 3))
    for group in (own[0], near[0][0], near[0][1], far_two):
        group.finish()
    coords[NB:2 * NB] = triple(factors[0], sums[0])
    wait(far)
    multiply(1, [(208, 16), (240, 16)], 8)
    tail.share_out()
    near[1][0].collect()
    far_one.exchange()
    gram_group.finish()
    around = [
        remote(gram.at[mine], gram.at[pl.ds(pl.multiple_of(away * 64 + k * SHARE, SHARE), SHARE)],
               gram_send.at[away], gram_recv.at[away], device)
        for away, device in ((3, up), (1, down), (2, across))
    ]
    two_at = coords.at[NB:2 * NB]
    near_two = local(two_at, y)
    turn(1, 0)
    tail.exchange()
    update(0, near_two, range(0, 3))
    near[1][1].collect()
    wait(around)
    swap = []
    for away in range(4):
        rows = pl.ds(pl.multiple_of(away * 64 + k * SHARE, SHARE), SHARE)
        swap.append(remote(gram.at[rows], gram.at[rows], gsib_send.at[away], gsib_recv.at[away], sibling))
    far_one.collect()
    update(0, near_two, range(3, 8))
    wait(swap)
    for away in range(4):
        home = lax.rem(y + away, NY)
        right_side[pl.ds(pl.multiple_of(home * 64, 64), 64)] = triple(gram[away * 64:(away + 1) * 64], local(two_at, home))
    tail.collect()
    turn(1, 1)
    for group in (own[1], near[1][0], near[1][1], far_one, tail):
        group.finish()
    coords[0:NB] = triple(factors[1], sums[1] - right_side[...])
    near_one[...] = local(coords.at[0:NB], y)
    for copy in sends:
        copy.wait_send()


CHUNKS = 8


def last_update(work, high, low, near_one, coords, updated, coords_out, stage, sem):
    copies = [pltpu.make_async_copy(coords, coords_out, sem.at[CHUNKS])]
    copies[0].start()
    ch, cl = split(near_one[...])
    size = ROWS // CHUNKS
    for i in range(CHUNKS):
        rows = slice(i * size, (i + 1) * size)
        h = high[rows]
        stage[rows] = work[rows] - (dot(h, ch) + dot(low[rows], ch) + dot(h, cl))
        copies.append(pltpu.make_async_copy(stage.at[rows], updated.at[rows], sem.at[i]))
        copies[-1].start()
    for copy in copies:
        copy.wait()


def shards(modes, panel_one, panel_two, factor_one, factor_two):
    hbm, vmem = pl.BlockSpec(memory_space=pltpu.HBM), pl.BlockSpec(memory_space=pltpu.VMEM)
    dma = pltpu.SemaphoreType.DMA
    state = pl.pallas_call(
        kernel,
        out_shape=(
            pltpu.VMEM((ROWS, COLS), F32), pltpu.VMEM((ROWS, NB), BF16), pltpu.VMEM((ROWS, NB), BF16),
            pltpu.VMEM((NB, COLS), F32), pltpu.VMEM((2 * NB, COLS), F32),
        ),
        in_specs=[hbm] * 5,
        out_specs=(vmem,) * 5,
        scratch_shapes=[
            pltpu.VMEM((2, NB, ROWS), F32),
            pltpu.VMEM((ROWS, COLS), BF16),
            pltpu.VMEM((ROWS, COLS), BF16),
            pltpu.VMEM((ROWS, NB), BF16),
            pltpu.VMEM((ROWS, NB), BF16),
            pltpu.VMEM((2, NB, NB), F32),
            pltpu.VMEM((13, 64, COLS), F32),
            pltpu.VMEM((13, NX, 16, COLS), F32),
            pltpu.VMEM((13, NZ, 16, COLS), F32),
            pltpu.VMEM((2, NB, COLS), F32),
            pltpu.VMEM((NB, NB), F32),
            pltpu.VMEM((NB, COLS), F32),
            dma((12,)),
            dma((2, 2, UNITS)), dma((2, 2, UNITS)),
            dma((2, 2, UNITS)), dma((2, 2, UNITS)),
            dma((2, 4, UNITS)), dma((2, 4, UNITS)),
            dma((13, NX - 1)), dma((13, NX - 1)),
            dma((13, NZ - 1)), dma((13, NZ - 1)),
            dma((13, NX - 1)), dma((13, NX - 1)),
            dma((4,)), dma((4,)),
            dma((4,)), dma((4,)),
        ],
        compiler_params=pltpu.CompilerParams(collective_id=0, has_side_effects=True, vmem_limit_bytes=54 << 20),
    )(modes, panel_one.T, panel_two.T, factor_one, factor_two)
    return pl.pallas_call(
        last_update,
        out_shape=(jax.ShapeDtypeStruct((ROWS, COLS), F32), jax.ShapeDtypeStruct((2 * NB, COLS), F32)),
        in_specs=[vmem] * 5,
        out_specs=(hbm, hbm),
        scratch_shapes=[pltpu.VMEM((ROWS, COLS), F32), dma((CHUNKS + 1,))],
        compiler_params=pltpu.CompilerParams(vmem_limit_bytes=24 << 20),
    )(*state)


def solution(mesh):
    return jax.shard_map(
        shards,
        mesh=mesh,
        in_specs=(P("row", "col"), P("row", "col"), P("row", "col"), P(), P()),
        out_specs=(P("row", "col"), P(None, "col")),
        check_vma=False,
    )
```
